512 devices in a mesh: seg: 16 (over z_hi, x, core), lat: 32 (over z_lo, y).
Axes of the slice: x: 4, y: 4, z: 16 (z_hi: 2, z_lo: 8; z = z_hi * 8 + z_lo), core: 2. Of those that a mesh axis runs over, the one named last changes fastest.
Arguments:
- states: bfloat16 [16, 256, 32, 1024], P('seg', 'lat'), may hold values from -20 to 20
- norm_gain: float32 [1024], replicated, may hold values from 0.1 to 1.9
- w_query: bfloat16 [1024, 512], replicated, may hold values from -1.5 to 1.5
- w_kv: bfloat16 [1024, 1024], replicated, may hold values from -1.5 to 1.5
- reach_rows: int32 [256], P('lat'), may hold values from 1 to 4, as said below
- mem_keep: int32 [16, 32], P('seg', 'lat'), may hold values from 0 to 1, as said below
- d_context: bfloat16 [16, 256, 32, 512], P('seg', 'lat'), may hold values from -6 to 6
Outputs:
- context: bfloat16 [16, 256, 32, 512], P('seg', 'lat')
- grad_states: bfloat16 [16, 256, 32, 1024], P('seg', 'lat')
The draws below stay inside these ranges and needn't reach their ends.
Inputs may be any that keep to these rules, and one draw needn't show every extreme that they name: `reach_rows`: 4 occurs in every draw. `mem_keep`: 1 where a band of a segment continues the record of its predecessor; among segments 1 to 15 every draw has some 0 and some 1.
All inputs are finite; a program needn't handle non-finite values.
Results may differ from the reference program's by a relative error of at most 0.023.
The reference program's roundings to bfloat16 on the way (of `normed`, `queries`, `keyval`, `probs`, `d_score` and `d_query`) count: a program that leaves them out, or rounds other values in their place, can miss the bound.
Values may be sent and summed in bfloat16 or wider, within the bound.
No kernel may reach another device: no remote copies, remote signals or barrier semaphores. Data moves between devices by JAX's collectives and lax.ppermute only.
A program may use at most 64 MiB of HBM per device.

```python
import jax
import jax.numpy as jnp
from jax import lax

D = 1024
HEADS = 8
HEAD_DIM = 64
LON = 32
ROWS_DEV = 8
HALO = 4
INNER = 512
SEGS = 16
BANDS = 32
LATROWS = 256


def draw_states(key, part):
    return jnp.clip(jax.random.normal(jax.random.fold_in(key, 4), (SEGS, LATROWS, LON, D), jnp.float32), -6.0, 6.0).astype(jnp.bfloat16)


def drawn_weight(key, salt):
    base = jax.random.normal(jax.random.fold_in(key, salt), (D, HEADS * HEAD_DIM), jnp.float32)
    return jnp.clip(base, -6.0, 6.0) * D ** (-0.5)


def draw_w_query(key, part):
    base = drawn_weight(key, 13)
    return base.astype(jnp.bfloat16)


def draw_w_kv(key, part):
    values = drawn_weight(key, 15)
    keys = drawn_weight(key, 14)
    return jnp.concatenate([keys, values], 1).astype(jnp.bfloat16)


def draw_reach_rows(key, part):
    base = jax.random.randint(jax.random.fold_in(key, 21), (LATROWS,), 1, HALO + 1)
    chosen = jax.random.randint(jax.random.fold_in(key, 22), (), 0, LATROWS)
    return jnp.where(jnp.arange(LATROWS) == chosen, HALO, base).astype(jnp.int32)


def draw_mem_keep(key, part):
    base = jax.random.randint(jax.random.fold_in(key, 31), (SEGS, BANDS), 0, 2)
    later = (SEGS - 1) * BANDS
    off_place = jax.random.randint(jax.random.fold_in(key, 32), (), 0, later)
    step = jax.random.randint(jax.random.fold_in(key, 33), (), 1, later)
    on_place = (off_place + step) % later
    places = jnp.arange(SEGS * BANDS).reshape(SEGS, BANDS) - BANDS
    base = jnp.where(places == off_place, 0, base)
    base = jnp.where(places == on_place, 1, base)
    return base.astype(jnp.int32)


def shard_levels(rng, shape, cuts, least, largest):
    gain, own = 1.0, jax.random.fold_in(rng, 6)
    for axis_at, parts in cuts:
        steps = jnp.exp(jax.random.uniform(jax.random.fold_in(own, axis_at), (parts,), jnp.float32, least / len(cuts), largest / len(cuts)))
        gain = gain * jnp.repeat(steps, shape[axis_at] // parts).reshape([-1 if axis == axis_at else 1 for axis in range(len(shape))])
    return gain


def gaussian(stream_key, shape, scale, limit, shards=(), held_as=jnp.bfloat16):
    array = scale * jax.random.normal(stream_key, shape, jnp.float32)
    if shards:
        array = array * shard_levels(stream_key, shape, shards, -0.22, 0.18)
    return jnp.clip(array, -limit, limit).astype(held_as)


def setup_inputs(seed: int = 0) -> dict:
    arg_keys = jax.random.split(jax.random.key(seed), 8)
    states = draw_states(jax.random.fold_in(arg_keys[7], 71), 0)
    norm_gain = jnp.clip(1.0 + 0.18 * jax.random.normal(arg_keys[1], (D,), jnp.float32), 0.1, 1.9)
    w_query = draw_w_query(jax.random.fold_in(arg_keys[7], 71), 0)
    w_kv = draw_w_kv(jax.random.fold_in(arg_keys[7], 71), 0)
    reach_rows = draw_reach_rows(jax.random.fold_in(arg_keys[7], 71), 0)
    mem_keep = draw_mem_keep(jax.random.fold_in(arg_keys[7], 71), 0)
    d_context = gaussian(arg_keys[6], (SEGS, LATROWS, LON, INNER), 1.0, 6.0, ((0, 16), (1, 32)))
    return dict(states=states, norm_gain=norm_gain, w_query=w_query, w_kv=w_kv, reach_rows=reach_rows, mem_keep=mem_keep, d_context=d_context)


NORM_EPS = 1e-06

def mix(form, left, right):
    return jnp.einsum(form, left.astype(jnp.float32), right.astype(jnp.float32))

def dot_back(left, weight):
    return jnp.dot(left, weight.T, preferred_element_type=jnp.float32)

def attend(queries, window, memory, reach_band, top_ok, bottom_ok, mem_ok, d_ctx):
    row_count, lon_count, inner_width = queries.shape
    key_rows = window.shape[0]
    halo_rows = (key_rows - row_count) // 2
    head_count = inner_width // HEAD_DIM
    tok_count = row_count * lon_count
    near_count = key_rows * lon_count
    query_tok = queries.reshape(tok_count, head_count, HEAD_DIM)
    joined = jnp.concatenate([window.reshape(near_count, 2 * inner_width), memory.reshape(tok_count, 2 * inner_width)], 0)
    key_tok = joined[:, :inner_width].reshape(-1, head_count, HEAD_DIM)
    value_tok = joined[:, inner_width:].reshape(-1, head_count, HEAD_DIM)
    query_row = jnp.arange(row_count, dtype=jnp.int32)[:, None]
    key_row = jnp.arange(key_rows, dtype=jnp.int32)[None, :]
    row_gap = key_row - halo_rows - query_row
    inside = (key_row >= halo_rows) | top_ok
    inside = inside & ((key_row < halo_rows + row_count) | bottom_ok)
    usable = (jnp.abs(row_gap) <= reach_band[:, None]) & inside
    near_mask = jnp.broadcast_to(usable[:, None, :, None], (row_count, lon_count, key_rows, lon_count)).reshape(tok_count, near_count)
    far_mask = jnp.broadcast_to(mem_ok, (tok_count, tok_count))
    allowed = jnp.concatenate([near_mask, far_mask], 1)
    scores = mix('qhd,khd->hqk', query_tok, key_tok) * HEAD_DIM ** (-0.5)
    scores = jnp.where(allowed[None], scores, -jnp.inf)
    row_max = lax.optimization_barrier(jnp.max(scores, axis=-1, keepdims=True))
    lifted = jnp.exp(scores - row_max)
    weights = lifted / lax.optimization_barrier(jnp.sum(lifted, axis=-1, keepdims=True))
    probs = weights.astype(jnp.bfloat16)
    context = mix('hqk,khd->qhd', probs, value_tok).astype(jnp.bfloat16)
    d_out = d_ctx.reshape(tok_count, head_count, HEAD_DIM)
    d_prob = mix('qhd,khd->hqk', d_out, value_tok)
    centre = lax.optimization_barrier(jnp.sum(weights * d_prob, axis=-1, keepdims=True))
    d_score = (weights * (d_prob - centre) * HEAD_DIM ** (-0.5)).astype(jnp.bfloat16)
    d_query = mix('hqk,khd->qhd', d_score, key_tok).astype(jnp.bfloat16)
    d_key = mix('hqk,qhd->khd', d_score[:, :, :near_count], query_tok).astype(jnp.bfloat16)
    d_value = mix('hqk,qhd->khd', probs[:, :, :near_count], d_out).astype(jnp.bfloat16)
    d_window = jnp.concatenate([d_key.reshape(near_count, inner_width), d_value.reshape(near_count, inner_width)], 1)
    return (context.reshape(row_count, lon_count, inner_width), d_query.reshape(row_count, lon_count, inner_width), d_window.reshape(key_rows, lon_count, 2 * inner_width))

def reference(states, norm_gain, w_query, w_kv, reach_rows, mem_keep, d_context):
    inner_width = w_query.shape[1]
    band_count = LATROWS // ROWS_DEV

    def project(slab):
        widened = slab.astype(jnp.float32)
        inv_rms = lax.rsqrt(lax.optimization_barrier(jnp.mean(widened * widened, axis=-1, keepdims=True)) + NORM_EPS)
        normed = (widened * inv_rms * norm_gain).astype(jnp.bfloat16)
        flat = normed.reshape(-1, D)
        queries = jnp.dot(flat, w_query, preferred_element_type=jnp.float32).astype(jnp.bfloat16)
        keyval = jnp.dot(flat, w_kv, preferred_element_type=jnp.float32).astype(jnp.bfloat16)
        return (queries.reshape(LATROWS, LON, inner_width), keyval.reshape(LATROWS, LON, 2 * inner_width))
    queries, keyval = lax.map(project, states)
    padded = jnp.pad(keyval, ((0, 0), (HALO, HALO), (0, 0), (0, 0)))
    seg_ids = jnp.repeat(jnp.arange(SEGS, dtype=jnp.int32), band_count)
    band_ids = jnp.tile(jnp.arange(band_count, dtype=jnp.int32), SEGS)

    def block(ids):
        seg_id, band_id = ids
        zero = seg_id * 0
        first = band_id * ROWS_DEV
        prior = jnp.maximum(seg_id - 1, 0)
        q_block = lax.dynamic_slice(queries, (seg_id, first, zero, zero), (1, ROWS_DEV, LON, inner_width))[0]
        window = lax.dynamic_slice(padded, (seg_id, first, zero, zero), (1, ROWS_DEV + 2 * HALO, LON, 2 * inner_width))[0]
        memory = lax.dynamic_slice(keyval, (prior, first, zero, zero), (1, ROWS_DEV, LON, 2 * inner_width))[0]
        reach_band = lax.dynamic_slice_in_dim(reach_rows, first, ROWS_DEV)
        d_block = lax.dynamic_slice(d_context, (seg_id, first, zero, zero), (1, ROWS_DEV, LON, inner_width))[0]
        keep_flag = lax.dynamic_slice(mem_keep, (seg_id, band_id), (1, 1))[0, 0]
        mem_ok = (seg_id >= 1) & (keep_flag == 1)
        return attend(q_block, window, memory, reach_band, band_id > 0, band_id < band_count - 1, mem_ok, d_block)
    context, d_query, d_window = lax.map(block, (seg_ids, band_ids))
    context = context.reshape(SEGS, LATROWS, LON, inner_width)
    d_query = d_query.reshape(SEGS, band_count, ROWS_DEV, LON, inner_width)
    d_window = d_window.reshape(SEGS, band_count, ROWS_DEV + 2 * HALO, LON, 2 * inner_width)
    d_near = d_window[:, :, HALO:HALO + ROWS_DEV]
    to_upper = d_window[:, :, :HALO]
    to_lower = d_window[:, :, HALO + ROWS_DEV:]
    from_lower = jnp.concatenate([to_upper[:, 1:], jnp.zeros_like(to_upper[:, :1])], 1)
    from_upper = jnp.concatenate([jnp.zeros_like(to_lower[:, :1]), to_lower[:, :-1]], 1)

    def backward(items):
        slab, dq_seg, near_seg, upper_seg, lower_seg = items
        main = dot_back(dq_seg.reshape(-1, inner_width), w_query) + dot_back(near_seg.reshape(-1, 2 * inner_width), w_kv)
        main = main.reshape(band_count, ROWS_DEV, LON, D)
        head_add = dot_back(upper_seg.reshape(-1, 2 * inner_width), w_kv).reshape(band_count, HALO, LON, D)
        tail_add = dot_back(lower_seg.reshape(-1, 2 * inner_width), w_kv).reshape(band_count, HALO, LON, D)
        d_normed = jnp.concatenate([main[:, :HALO] + head_add, main[:, HALO:ROWS_DEV - HALO], main[:, ROWS_DEV - HALO:] + tail_add], 1)
        d_normed = d_normed.reshape(LATROWS, LON, D)
        widened = slab.astype(jnp.float32)
        inv_rms = lax.rsqrt(lax.optimization_barrier(jnp.mean(widened * widened, axis=-1, keepdims=True)) + NORM_EPS)
        scaled = d_normed * norm_gain
        grad = inv_rms * scaled - widened * inv_rms ** 3 * lax.optimization_barrier(jnp.mean(scaled * widened, axis=-1, keepdims=True))
        return grad.astype(jnp.bfloat16)
    grad_states = lax.map(backward, (states, d_query, d_near, from_upper, from_lower))
    return (context, grad_states)
```

```python
import jax
import jax.numpy as jnp
from jax import lax
from jax.experimental import pallas as pl
from jax.experimental.pallas import tpu as pltpu
from jax.sharding import PartitionSpec as P

HEAD_DIM = 64
HALO = 4
NORM_EPS = 1e-06
NEG = -1e30
BF = jnp.bfloat16
F32 = jnp.float32
VMEM_LIMIT = 40 * 1024 * 1024


def dot(a, b):
    return lax.dot_general(a, b, (((1,), (0,)), ((), ())), preferred_element_type=F32)


def dot_nt(a, b):
    return lax.dot_general(a, b, (((1,), (1,)), ((), ())), preferred_element_type=F32)


def inv_rms_of(wide):
    return lax.rsqrt(jnp.mean(wide * wide, axis=-1, keepdims=True) + NORM_EPS)


def project_kernel(states_ref, gain_ref, wq_ref, wkv_ref, q_ref, kv_ref):
    wide = states_ref[...].astype(F32)
    normed = (wide * inv_rms_of(wide) * gain_ref[...]).astype(BF)
    kv_ref[...] = dot(normed, wkv_ref[...]).astype(BF)
    q_ref[...] = dot(normed, wq_ref[...]).astype(BF)


def project(states, gain, w_query, w_kv):
    toks, width = states.shape
    inner = w_query.shape[1]
    return pl.pallas_call(
        project_kernel,
        out_shape=(
            jax.ShapeDtypeStruct((toks, inner), BF),
            jax.ShapeDtypeStruct((toks, 2 * inner), BF),
        ),
        compiler_params=pltpu.CompilerParams(vmem_limit_bytes=VMEM_LIMIT),
        cost_estimate=pl.CostEstimate(
            flops=6 * toks * width * inner, bytes_accessed=6 * width * inner, transcendentals=0
        ),
        name="project",
    )(states, gain, w_query, w_kv)


def bias_of(reach_ref, keep_ref, toks, lon):
    row = lax.broadcasted_iota(jnp.int32, (128, toks), 0)
    own = lax.broadcasted_iota(jnp.int32, (128, toks), 1) // lon
    reach = jnp.zeros((128, toks), jnp.int32)
    for i in range(2 * HALO):
        reach = jnp.where(own == i, reach_ref[i], reach)
    seg, band = lax.axis_index("seg"), lax.axis_index("lat")
    low = jnp.where(band > 0, 0, HALO)
    high = jnp.where(band < lax.axis_size("lat") - 1, 4 * HALO, 3 * HALO)
    mem_bias = jnp.where((seg >= 1) & (keep_ref[0] == 1), 0.0, NEG)
    usable = (jnp.abs(row - HALO - own) <= reach) & (row >= low) & (row < high)
    bias = jnp.where(usable, 0.0, NEG)
    bias = jnp.where(row == 4 * HALO, mem_bias, bias)
    return jnp.where(row > 4 * HALO, 0.0, bias).astype(BF)


def marked(keys, first, lon):
    count = keys.shape[0]
    col = lax.broadcasted_iota(jnp.int32, (count, 128), 1)
    if first == 4 * HALO:
        hot = col == first
    else:
        hot = col == first + lax.broadcasted_iota(jnp.int32, (count, 128), 0) // lon
    return jnp.concatenate([keys, jnp.where(hot, 1.0, 0.0).astype(BF)], axis=1)


def head_rows(h):
    return slice(h * HEAD_DIM, (h + 1) * HEAD_DIM)


def only_head(value, h):
    lane = lax.broadcasted_iota(jnp.int32, value.shape, 1)
    mine = (lane >= h * HEAD_DIM) & (lane < (h + 1) * HEAD_DIM)
    return jnp.where(mine, value, jnp.zeros_like(value))


def padded_t(value_t, h, below=()):
    zeros = jnp.zeros((HEAD_DIM, value_t.shape[1]), value_t.dtype)
    pieces = [zeros, zeros]
    pieces[h] = value_t[head_rows(h)]
    return jnp.concatenate(pieces + list(below), axis=0)


def halves(left_up, left_dn, right):
    half = right.shape[1] // 2
    return jnp.concatenate([dot(left_up, right[:, :half]), dot(left_dn, right[:, half:])], axis=1)


def window_kernel(
    reach_ref, keep_ref,
    q_ref, k_ref, v_ref, ku_ref, vu_ref, kd_ref, vd_ref, do_ref,
    ctx_ref, stats_ref, e_ref, d_ref,
):
    toks = q_ref.shape[0]
    half = toks // 2
    lon = half // HALO
    bias = bias_of(reach_ref, keep_ref, toks, lon)
    kx_own = marked(k_ref[...], HALO, lon)
    kx_up, kx_dn = marked(ku_ref[...], 0, lon), marked(kd_ref[...], 3 * HALO, lon)
    v_up, v_dn = vu_ref[...], vd_ref[...]
    q_t, do_t = (q_ref[...] * jnp.asarray(HEAD_DIM ** (-0.5), BF)).T, do_ref[...].T
    vt_own, vt_up, vt_dn = v_ref[...].T, v_up.T, v_dn.T
    for h in range(2):
        rows = head_rows(h)
        qt_h = padded_t(q_t, h, (bias,))
        s_own, s_halo = dot(kx_own, qt_h), halves(kx_up, kx_dn, qt_h)
        d_ref[h] = halves(v_up, v_dn, padded_t(do_t, h))
        top = jnp.maximum(jnp.max(s_own, axis=0, keepdims=True), jnp.max(s_halo, axis=0, keepdims=True))
        e_own, e_halo = jnp.exp(s_own - top), jnp.exp(s_halo - top)
        e_ref[h] = e_halo
        total = jnp.sum(e_own, axis=0, keepdims=True) + jnp.sum(e_halo, axis=0, keepdims=True)
        stats_ref[0, 2 * h : 2 * h + 2, :] = jnp.concatenate([top, total], axis=0)
        ctx_ref[rows] = dot(vt_own[rows], e_own.astype(BF)) + halves(vt_up[rows], vt_dn[rows], e_halo.astype(BF))


def outer_kernel(
    keep_ref,
    q_ref, km_ref, vm_ref, do_ref, part_ref, window_ref, e_ref, d_ref,
    ctx_ref, stats_ref, g_ref, dup_ref, ddn_ref,
):
    toks = q_ref.shape[0]
    half = toks // 2
    mem_bias = jnp.where((lax.axis_index("seg") >= 1) & (keep_ref[0] == 1), 0.0, NEG)
    bias = jnp.where(lax.broadcasted_iota(jnp.int32, (128, toks), 0) == 4 * HALO, mem_bias, 0.0).astype(BF)
    kx_mem = marked(km_ref[...], 4 * HALO, half // HALO)
    q = q_ref[...] * jnp.asarray(HEAD_DIM ** (-0.5), BF)
    d_out = do_ref[...]
    q_t, do_t, vt_mem = q.T, d_out.T, vm_ref[...].T
    sums = None
    ctx_parts = []
    for h in range(2):
        rows = head_rows(h)
        s_mem = dot(kx_mem, padded_t(q_t, h, (bias,)))
        before, part = window_ref[0, 2 * h : 2 * h + 1, :], window_ref[0, 2 * h + 1 : 2 * h + 2, :]
        top = jnp.maximum(jnp.max(s_mem, axis=0, keepdims=True), before)
        e_mem = jnp.exp(s_mem - top)
        fade = jnp.exp(before - top)
        inv = 1.0 / (part * fade + jnp.sum(e_mem, axis=0, keepdims=True))
        fade = fade * inv
        ctx_t = part_ref[rows] * fade + dot(vt_mem[rows], (e_mem * inv).astype(BF))
        centre = jnp.sum(ctx_t * do_t[rows].astype(F32), axis=0, keepdims=True)
        w_halo = e_ref[h] * fade
        p_halo = w_halo.astype(BF)
        g_halo = (w_halo * (d_ref[h] - centre)).astype(BF)
        stats_ref[0, 3 * h : 3 * h + 3, :] = jnp.concatenate([top, inv, centre], axis=0)
        g_ref[h] = g_halo
        ctx_parts.append(ctx_t)
        q_h, do_h = only_head(q, h), only_head(d_out, h)
        terms = (
            dot(g_halo[:, :half], q_h[:half]), dot(p_halo[:, :half], do_h[:half]),
            dot(g_halo[:, half:], q_h[half:]), dot(p_halo[:, half:], do_h[half:]),
        )
        sums = terms if sums is None else tuple(x + y for x, y in zip(sums, terms))
    dup_ref[0] = sums[0].astype(BF)
    dup_ref[1] = sums[1].astype(BF)
    ddn_ref[0] = sums[2].astype(BF)
    ddn_ref[1] = sums[3].astype(BF)
    ctx_ref[...] = jnp.concatenate(ctx_parts, axis=0).T.astype(BF)


def inner_kernel(
    reach_ref, keep_ref,
    q_ref, k_ref, v_ref, ku_ref, kd_ref, km_ref, vm_ref, do_ref, stats_ref, g_ref,
    dq_ref, dnear_ref,
):
    toks = q_ref.shape[0]
    lon = toks // (2 * HALO)
    scale = HEAD_DIM ** (-0.5)
    bias = bias_of(reach_ref, keep_ref, toks, lon)
    k_own, k_mem, v_own, v_mem = k_ref[...], km_ref[...], v_ref[...], vm_ref[...]
    kx_own, kx_mem = marked(k_own, HALO, lon), marked(k_mem, 4 * HALO, lon)
    q = q_ref[...] * jnp.asarray(scale, BF)
    d_out = do_ref[...]
    q_t, do_t = q.T, d_out.T
    kt_own, kt_up, kt_dn, kt_mem = k_own.T, ku_ref[...].T, kd_ref[...].T, k_mem.T
    sums = None
    dq_parts = []
    for h in range(2):
        rows = head_rows(h)
        qt_h = padded_t(q_t, h, (bias,))
        dot_h = padded_t(do_t, h)
        top, inv, centre = (stats_ref[0, 3 * h + i : 3 * h + i + 1, :] for i in range(3))
        w_own = jnp.exp(dot(kx_own, qt_h) - top) * inv
        w_mem = jnp.exp(dot(kx_mem, qt_h) - top) * inv
        g_own = (w_own * (dot(v_own, dot_h) - centre)).astype(BF)
        g_mem = (w_mem * (dot(v_mem, dot_h) - centre)).astype(BF)
        dq_parts.append(
            (dot(kt_own[rows], g_own) + dot(kt_mem[rows], g_mem) + halves(kt_up[rows], kt_dn[rows], g_ref[h]))
            * scale
        )
        terms = dot(g_own, only_head(q, h)), dot(w_own.astype(BF), only_head(d_out, h))
        sums = terms if sums is None else tuple(x + y for x, y in zip(sums, terms))
    dq_ref[...] = jnp.concatenate(dq_parts, axis=0).T.astype(BF)
    dnear_ref[0] = sums[0].astype(BF)
    dnear_ref[1] = sums[1].astype(BF)


def cols(count, shift):
    return pl.BlockSpec((count, 128), lambda i, *_: (0, i + shift))


def lead(lead_count, count, width):
    if width == 128:
        return pl.BlockSpec((lead_count, count, width), lambda i, *_: (0, 0, i))
    return pl.BlockSpec((lead_count, count, width), lambda i, *_: (i, 0, 0))


def attend_window(reach, keep, queries, keyval, halo, d_ctx):
    toks, inner = queries.shape
    half = toks // 2
    pairs = inner // 128
    up = lambda shift: pl.BlockSpec((half, 128), lambda i, *_: (0, i + shift))
    down = lambda shift: pl.BlockSpec((half, 128), lambda i, *_: (1, i + shift))
    return pl.pallas_call(
        window_kernel,
        grid_spec=pltpu.PrefetchScalarGridSpec(
            num_scalar_prefetch=2,
            grid=(pairs,),
            in_specs=[
                cols(toks, 0), cols(toks, 0), cols(toks, pairs),
                up(0), up(pairs), down(0), down(pairs), cols(toks, 0),
            ],
            out_specs=[
                pl.BlockSpec((128, toks), lambda i, *_: (i, 0)),
                lead(1, 8, toks), lead(2, half, toks), lead(2, half, toks),
            ],
        ),
        out_shape=(
            jax.ShapeDtypeStruct((inner, toks), F32),
            jax.ShapeDtypeStruct((pairs, 8, toks), F32),
            jax.ShapeDtypeStruct((2 * pairs, half, toks), F32),
            jax.ShapeDtypeStruct((2 * pairs, half, toks), F32),
        ),
        compiler_params=pltpu.CompilerParams(vmem_limit_bytes=VMEM_LIMIT),
        cost_estimate=pl.CostEstimate(
            flops=24 * toks * toks * inner, bytes_accessed=4 * toks * inner * 10, transcendentals=toks * toks * 16
        ),
        name="attend_window",
    )(reach, keep, queries, keyval, keyval, halo, halo, halo, halo, d_ctx)


def attend_outer(keep, queries, memory, d_ctx, part, window, e_halo, d_halo):
    toks, inner = queries.shape
    half = toks // 2
    pairs = inner // 128
    return pl.pallas_call(
        outer_kernel,
        grid_spec=pltpu.PrefetchScalarGridSpec(
            num_scalar_prefetch=1,
            grid=(pairs,),
            in_specs=[
                cols(toks, 0), cols(toks, 0), cols(toks, pairs), cols(toks, 0),
                pl.BlockSpec((128, toks), lambda i, *_: (i, 0)),
                lead(1, 8, toks), lead(2, half, toks), lead(2, half, toks),
            ],
            out_specs=[
                cols(toks, 0), lead(1, 8, toks), lead(2, half, toks), lead(2, half, 128), lead(2, half, 128),
            ],
        ),
        out_shape=(
            jax.ShapeDtypeStruct((toks, inner), BF),
            jax.ShapeDtypeStruct((pairs, 8, toks), F32),
            jax.ShapeDtypeStruct((2 * pairs, half, toks), BF),
            jax.ShapeDtypeStruct((2, half, inner), BF),
            jax.ShapeDtypeStruct((2, half, inner), BF),
        ),
        compiler_params=pltpu.CompilerParams(vmem_limit_bytes=VMEM_LIMIT),
        cost_estimate=pl.CostEstimate(
            flops=12 * toks * toks * inner, bytes_accessed=4 * toks * inner * 10, transcendentals=toks * toks * 8
        ),
        name="attend_outer",
    )(keep, queries, memory, memory, d_ctx, part, window, e_halo, d_halo)


def attend_inner(reach, keep, queries, keyval, halo, memory, d_ctx, stats, g_halo):
    toks, inner = queries.shape
    half = toks // 2
    pairs = inner // 128
    up = pl.BlockSpec((half, 128), lambda i, *_: (0, i))
    down = pl.BlockSpec((half, 128), lambda i, *_: (1, i))
    return pl.pallas_call(
        inner_kernel,
        grid_spec=pltpu.PrefetchScalarGridSpec(
            num_scalar_prefetch=2,
            grid=(pairs,),
            in_specs=[
                cols(toks, 0), cols(toks, 0), cols(toks, pairs), up, down,
                cols(toks, 0), cols(toks, pairs), cols(toks, 0), lead(1, 8, toks), lead(2, half, toks),
            ],
            out_specs=[cols(toks, 0), lead(2, toks, 128)],
        ),
        out_shape=(
            jax.ShapeDtypeStruct((toks, inner), BF),
            jax.ShapeDtypeStruct((2, toks, inner), BF),
        ),
        compiler_params=pltpu.CompilerParams(vmem_limit_bytes=VMEM_LIMIT),
        cost_estimate=pl.CostEstimate(
            flops=24 * toks * toks * inner, bytes_accessed=4 * toks * inner * 10, transcendentals=toks * toks * 16
        ),
        name="attend_inner",
    )(reach, keep, queries, keyval, keyval, halo, halo, memory, memory, d_ctx, stats, g_halo)


def main_back_kernel(dq_ref, dnear_ref, wq_ref, wkv_ref, out_ref):
    inner = dq_ref.shape[1]
    out_ref[...] = (
        dot_nt(dq_ref[...], wq_ref[...])
        + dot_nt(dnear_ref[0], wkv_ref[:, :inner])
        + dot_nt(dnear_ref[1], wkv_ref[:, inner:])
    )


def main_back(d_query, d_near, w_query, w_kv):
    toks, inner = d_query.shape
    width = w_query.shape[0]
    return pl.pallas_call(
        main_back_kernel,
        out_shape=jax.ShapeDtypeStruct((toks, width), F32),
        compiler_params=pltpu.CompilerParams(vmem_limit_bytes=VMEM_LIMIT),
        cost_estimate=pl.CostEstimate(
            flops=6 * toks * width * inner, bytes_accessed=6 * width * inner, transcendentals=0
        ),
        name="main_back",
    )(d_query, d_near, w_query, w_kv)


def finish_kernel(main_ref, low_ref, high_ref, states_ref, gain_ref, wkv_ref, out_ref):
    inner = low_ref.shape[2]
    d_keys = jnp.concatenate([low_ref[0], high_ref[0]], axis=0)
    d_values = jnp.concatenate([low_ref[1], high_ref[1]], axis=0)
    d_normed = main_ref[...] + dot_nt(d_keys, wkv_ref[:, :inner]) + dot_nt(d_values, wkv_ref[:, inner:])
    wide = states_ref[...].astype(F32)
    inv = inv_rms_of(wide)
    scaled = d_normed * gain_ref[...]
    mean = jnp.mean(scaled * wide, axis=-1, keepdims=True)
    out_ref[...] = (inv * scaled - wide * (inv * inv * inv * mean)).astype(BF)


def finish(main, low, high, states, gain, w_kv):
    toks, width = states.shape
    return pl.pallas_call(
        finish_kernel,
        out_shape=jax.ShapeDtypeStruct((toks, width), BF),
        compiler_params=pltpu.CompilerParams(vmem_limit_bytes=VMEM_LIMIT),
        cost_estimate=pl.CostEstimate(
            flops=4 * toks * width * low.shape[2], bytes_accessed=6 * toks * width, transcendentals=0
        ),
        name="finish",
    )(main, low, high, states, gain, w_kv)


def normed_of(states, gain):
    wide = states.astype(F32)
    return (wide * inv_rms_of(wide) * gain).astype(BF)


def halo_kernel(up_ref, down_ref, late_up_ref, late_down_ref, gain_ref, wkv_ref, out_ref):
    waits = lax.axis_index("seg") == lax.axis_size("seg") // 2
    up = jnp.where(waits, late_up_ref[...], up_ref[...])
    down = jnp.where(waits, late_down_ref[...], down_ref[...])
    normed = normed_of(jnp.concatenate([up, down], axis=0), gain_ref[...])
    out_ref[...] = dot(normed, wkv_ref[...]).astype(BF)


def project_halo(up, down, late_up, late_down, gain, w_kv):
    edge, width = up.shape
    double = w_kv.shape[1]
    return pl.pallas_call(
        halo_kernel,
        out_shape=jax.ShapeDtypeStruct((2 * edge, double), BF),
        compiler_params=pltpu.CompilerParams(vmem_limit_bytes=VMEM_LIMIT),
        cost_estimate=pl.CostEstimate(
            flops=4 * edge * width * double, bytes_accessed=4 * width * double, transcendentals=0
        ),
        name="project_halo",
    )(up, down, late_up, late_down, gain, w_kv)


def route():
    seg, band = lax.axis_index("seg"), lax.axis_index("lat")
    last = lax.axis_size("seg") // 2 - 1
    group = (band // 4) % 4
    relay_seg = jnp.where(group == 0, -1, 2 * group - 2)
    relays = seg == relay_seg
    sends = seg == jnp.where(group == 0, last, jnp.where(group == 1, -1, relay_seg - 1))
    late = (seg == last + 1) | (relays & (seg > 0))
    return relays, sends, late


def across_kernel(early_ref, own_ref, out_ref, held, sem):
    relays, sends, _ = route()

    def pass_on(source):
        copy_in = pltpu.make_async_copy(source, held, sem)
        copy_in.start()
        copy_in.wait()
        copy_out = pltpu.make_async_copy(held, out_ref, sem)
        copy_out.start()
        copy_out.wait()

    @pl.when(relays)
    def _():
        pass_on(early_ref)

    @pl.when(sends)
    def _():
        pass_on(own_ref)


def across_of(early, own):
    anywhere = pl.BlockSpec(memory_space=pl.ANY)
    return pl.pallas_call(
        across_kernel,
        in_specs=[anywhere, anywhere],
        out_specs=anywhere,
        out_shape=jax.ShapeDtypeStruct(own.shape, own.dtype),
        scratch_shapes=[pltpu.VMEM(own.shape, own.dtype), pltpu.SemaphoreType.DMA],
        name="across",
    )(early, own)


def edges_kernel(own_ref, up_ref, down_ref):
    edge = up_ref.shape[0]
    toks = own_ref.shape[0]
    up_ref[...] = own_ref[toks - edge :, :]
    down_ref[...] = own_ref[:edge, :]


def edges_of(own, edge):
    return pl.pallas_call(
        edges_kernel,
        out_shape=(jax.ShapeDtypeStruct((edge, own.shape[1]), own.dtype),) * 2,
        name="edges",
    )(own)


def memory_kernel(early_ref, late_ref, gain_ref, wkv_ref, out_ref, held, sem):
    _, _, late = route()

    @pl.when(late)
    def _():
        copy = pltpu.make_async_copy(late_ref, held, sem)
        copy.start()
        copy.wait()

    @pl.when(jnp.logical_not(late))
    def _():
        copy = pltpu.make_async_copy(early_ref, held, sem)
        copy.start()
        copy.wait()

    out_ref[...] = dot(normed_of(held[...], gain_ref[...]), wkv_ref[...]).astype(BF)


def project_memory(early, late, gain, w_kv):
    toks, width = early.shape
    double = w_kv.shape[1]
    vmem = pl.BlockSpec(memory_space=pltpu.VMEM)
    anywhere = pl.BlockSpec(memory_space=pl.ANY)
    return pl.pallas_call(
        memory_kernel,
        in_specs=[anywhere, anywhere, vmem, vmem],
        out_shape=jax.ShapeDtypeStruct((toks, double), BF),
        scratch_shapes=[pltpu.VMEM((toks, width), BF), pltpu.SemaphoreType.DMA],
        compiler_params=pltpu.CompilerParams(vmem_limit_bytes=VMEM_LIMIT),
        cost_estimate=pl.CostEstimate(
            flops=2 * toks * width * double, bytes_accessed=4 * width * double, transcendentals=0
        ),
        name="project_memory",
    )(early, late, gain, w_kv)


def shifted(value, axis, by):
    count = lax.axis_size(axis)
    pairs = [(i, i + by) for i in range(count) if 0 <= i + by < count]
    return lax.ppermute(value, axis, pairs)


def shifted_in(value, by, segs, bands, chosen):
    pairs = [
        (seg * bands + i, seg * bands + i + by)
        for seg in range(segs) if chosen(seg)
        for i in range(bands) if 0 <= i + by < bands
    ]
    return lax.ppermute(value, ("seg", "lat"), pairs)


def memory_routes(segs, bands):
    last = segs // 2 - 1
    relays = (last, 0, 2, 4)
    first, second = [], []
    for band in range(bands):
        relay = relays[(band // 4) % 4]
        for seg in range(segs - 1):
            pair = (seg * bands + band, (seg + 1) * bands + band)
            if seg == last:
                if relay != last:
                    first.append((pair[0], relay * bands + band))
                second.append((relay * bands + band, pair[1]))
            elif seg + 1 == relay and relay != last:
                second.append(pair)
            else:
                first.append(pair)
    return first, second


def body(states, norm_gain, w_query, w_kv, reach_rows, mem_keep, d_context):
    _, rows, lon, width = states.shape
    inner = w_query.shape[1]
    toks = rows * lon
    edge = HALO * lon
    flat = states.reshape(toks, width)
    gain = norm_gain.reshape(1, width)
    first, second = memory_routes(lax.axis_size("seg"), lax.axis_size("lat"))
    d_ctx = d_context.reshape(toks, inner)
    keep = mem_keep.reshape(1)
    segs, bands = lax.axis_size("seg"), lax.axis_size("lat")
    early, after = (lambda seg: seg != segs // 2), (lambda seg: seg == segs // 2)
    early_mem = lax.ppermute(flat, ("seg", "lat"), first)
    upper, lower = edges_of(flat, edge)
    up_states = shifted_in(upper, 1, segs, bands, early)
    down_states = shifted_in(lower, -1, segs, bands, early)
    across = across_of(early_mem, flat)
    across, own = lax.optimization_barrier((across, flat))
    late_mem = lax.ppermute(across, ("seg", "lat"), second)
    queries, keyval = project(own, gain, w_query, w_kv)
    up_states, down_states, upper, lower, queries, keyval = lax.optimization_barrier(
        (up_states, down_states, upper, lower, queries, keyval)
    )
    late_up = shifted_in(upper, 1, segs, bands, after)
    late_down = shifted_in(lower, -1, segs, bands, after)
    halo = project_halo(up_states, down_states, late_up, late_down, gain, w_kv)
    part, window, e_halo, d_halo = attend_window(reach_rows, keep, queries, keyval, halo, d_ctx)
    memory = project_memory(early_mem, late_mem, gain, w_kv)
    context, stats, g_halo, d_up, d_down = attend_outer(
        keep, queries, memory, d_ctx, part, window, e_halo, d_halo
    )
    high = shifted(d_up, "lat", -1)
    low = shifted(d_down, "lat", 1)
    d_query, d_near = attend_inner(
        reach_rows, keep, queries, keyval, halo, memory, d_ctx, stats, g_halo
    )
    main = main_back(d_query, d_near, w_query, w_kv)
    grad = finish(main, low, high, flat, gain, w_kv)
    return (
        context.reshape(1, rows, lon, inner),
        grad.reshape(1, rows, lon, width),
    )


def solution(mesh):
    tokens = P("seg", "lat", None, None)
    return jax.shard_map(
        body,
        mesh=mesh,
        in_specs=(tokens, P(), P(), P(), P("lat"), P("seg", "lat"), tokens),
        out_specs=(tokens, tokens),
        check_vma=False,
    )
```
